32 devices in a mesh: row: 4 (over y, x), col: 8 (over z, core).
Axes of the slice: x: 2, y: 2, z: 4, core: 2. Of those that a mesh axis runs over, the one named last changes fastest.
Arguments:
- pair_tensor: bfloat16 [1024, 1024, 128], P('row', 'col'), may hold values from -6 to 6
- token_single: bfloat16 [1024, 768], P('row'), may hold values from -6 to 6
- atom_single: bfloat16 [8192, 128], P(('row', 'col')), may hold values from -6 to 6
- atom_token: int32 [8192], replicated, may hold values from 0 to 1023, as said below
- chain_index: int32 [1024], replicated, may hold values from 0 to 15, never falling along the last dimension, each value on 1 to 256 neighbouring positions
- pair_up: bfloat16 [128, 512], replicated, may hold values from -0.5 to 0.5
- pair_down: bfloat16 [256, 128], replicated, may hold values from -0.75 to 0.75
- bias_heads: bfloat16 [128, 20], replicated, may hold values from -0.5 to 0.5
- atom_gain: float32 [128], replicated, may hold values from 0.1 to 1.9
- atom_proj: bfloat16 [128, 512], replicated, may hold values from -0.5 to 0.5
- atom_exit: bfloat16 [128, 128], replicated, may hold values from -0.5 to 0.5
- atom_pool: bfloat16 [128, 768], replicated, may hold values from -0.5 to 0.5
- token_gain: float32 [768], replicated, may hold values from 0.1 to 1.9
- token_proj: bfloat16 [768, 3072], replicated, may hold values from -0.21875 to 0.21875
- token_exit: bfloat16 [768, 768], replicated, may hold values from -0.21875 to 0.21875
- chain_bias: float32 [16], replicated, may hold values from -2 to 115
- token_back: bfloat16 [768, 128], replicated, may hold values from -0.21875 to 0.21875
Outputs:
- token_update: bfloat16 [1024, 768], P('row')
- atom_update: bfloat16 [8192, 128], P(('row', 'col'))
The draws below stay inside these ranges and needn't reach their ends.
Inputs may be any that keep to these rules, and one draw needn't show every extreme that they name: `atom_token`: Non-decreasing. For every r, the atoms r * 8 * 256 to (r + 1) * 8 * 256 - 1 belong to the tokens r * 256 to (r + 1) * 256 - 1, and every token has one atom or more.
All inputs are finite; a program needn't handle non-finite values.
Results may differ from the reference program's by a relative error of at most 0.0085.
Values may be sent and summed in bfloat16 or wider, within the bound.
A program may use at most 128 MiB of HBM per device.

```python
import math
import jax
import jax.numpy as jnp
import numpy as np
from jax import lax

CZ = 128
CS = 768
CA = 128
HT = 16
HA = 4
PH = 256
QB = 32
KW = 128
APT = 8
CHAINS = 16
TOK_R = 256
TOKENS = 1024
ATOMS = 8192
EDGE = 48
HDA = 32
HDT = 48
HB = 20


def draw_atom_token(key, part):
    key = jax.random.fold_in(key, 11)
    groups = TOKENS // TOK_R
    spare = APT * TOK_R - TOK_R
    key_one, key_two, key_three = jax.random.split(key, 3)
    first_pick = jax.random.randint(key_one, (groups, spare), 0, TOK_R)
    second_pick = jax.random.randint(key_two, (groups, spare), 0, TOK_R)
    coin_flip = jax.random.randint(key_three, (groups, spare), 0, 2)
    extra = jnp.where(coin_flip == 1, jnp.minimum(first_pick, second_pick), first_pick).astype(jnp.int32)
    base_tokens = jnp.broadcast_to(jnp.arange(TOK_R, dtype=jnp.int32)[None, :], (groups, TOK_R))
    local_tokens = jnp.sort(jnp.concatenate([base_tokens, extra], axis=1), axis=1)
    offsets = (jnp.arange(groups, dtype=jnp.int32) * TOK_R)[:, None]
    return (local_tokens + offsets).reshape(-1).astype(jnp.int32)


def chain_values(key, big_lo, big_hi):
    key_order, key_small, key_big = jax.random.split(key, 3)
    order = jax.random.permutation(key_order, HT)
    strong = order < HT // 2
    small_part = jax.random.uniform(key_small, (HT,), jnp.float32, -2.0, 2.0)
    big_part = jax.random.uniform(key_big, (HT,), jnp.float32, big_lo, big_hi)
    return jnp.where(strong, big_part, small_part).astype(jnp.float32)


def draw_chain_bias(key, part):
    key = jax.random.fold_in(key, 23)
    return chain_values(key, 96.0, 110.0)


def shard_levels(rng, dims, cuts, low, largest):
    factor_of = 1.0
    for position, shards_of in cuts:
        draws = jax.random.uniform(jax.random.fold_in(jax.random.fold_in(rng, 6), position), (shards_of,), jnp.float32, low / len(cuts), largest / len(cuts))
        factor_of = factor_of * jnp.repeat(jnp.exp(draws), dims[position] // shards_of).reshape((-1,) + (1,) * (len(dims) - 1 - position))
    return factor_of


def split_up(amount, total, limit, slope):
    portions = [(1 << 20) // math.isqrt(standing ** slope) + 1 for standing in range(2, amount + 1)]
    rest, given = total - limit - (amount - 1), [1] * (amount - 1)
    while rest > 0:
        free = [i for i in range(amount - 1) if given[i] < limit]
        mass, left = sum([portions[i] for i in free]), rest
        for i in free:
            addition = min(limit - given[i], max(1, left * portions[i] // mass), rest)
            given[i] = given[i] + addition
            rest = rest - addition
    return np.array([limit] + given)


def ragged_sizes(own_key, count, total, bound, lean):
    if count == 2:
        one = jax.random.randint(own_key, (), max(1, total - bound), min(bound, total - 1) + 1)
        return jnp.stack([one, total - one])
    tallies = jnp.asarray(split_up(count, total, bound, lean), jnp.int32)
    pairs = (count - 1) // 2
    giver, taker = tallies[1:1 + 2 * pairs:2], tallies[2:2 + 2 * pairs:2]
    room = jnp.minimum(giver - 1, bound - taker)
    shifted = jax.random.randint(jax.random.fold_in(own_key, 1), (pairs,), 0, 1 << 20) % (room + 1)
    tallies = tallies.at[1:1 + 2 * pairs:2].set(giver - shifted).at[2:2 + 2 * pairs:2].set(taker + shifted)
    return tallies[jax.random.permutation(jax.random.fold_in(own_key, 2), count)]


def gaussian(key, shape, scale, reach, cuts=(), kind=jnp.bfloat16):
    drawn = scale * jax.random.normal(key, shape, jnp.float32)
    if cuts:
        drawn = drawn * shard_levels(key, shape, cuts, -0.22, 0.18)
    return jnp.clip(drawn, -reach, reach).astype(kind)


def setup_inputs(seed: int = 0) -> dict:
    arg_keys = jax.random.split(jax.random.key(seed), 18)
    return {
        "pair_tensor": gaussian(arg_keys[0], (TOKENS, TOKENS, CZ), 1.0, 6.0, ((0, 4), (1, 8))),
        "token_single": gaussian(arg_keys[1], (TOKENS, CS), 1.0, 6.0, ((0, 4),)),
        "atom_single": gaussian(arg_keys[2], (ATOMS, CA), 1.0, 6.0, ((0, 32),)),
        "atom_token": draw_atom_token(jax.random.fold_in(arg_keys[17], 71), 0),
        "chain_index": jnp.searchsorted(jnp.cumsum(ragged_sizes(arg_keys[4], CHAINS, TOKENS, TOKENS // 4, 1)), jnp.arange(TOKENS), side="right").astype(jnp.int32),
        "pair_up": gaussian(arg_keys[5], (CZ, 2 * PH), CZ ** -0.5, 0.5),
        "pair_down": gaussian(arg_keys[6], (PH, CZ), (PH // 4) ** -0.5, 0.75),
        "bias_heads": gaussian(arg_keys[7], (CZ, HB), CZ ** -0.5, 0.5),
        "atom_gain": jnp.clip(1.0 + 0.18 * jax.random.normal(arg_keys[8], (CA,), jnp.float32), 0.1, 1.9),
        "atom_proj": gaussian(arg_keys[9], (CA, 4 * CA), CA ** -0.5, 0.5),
        "atom_exit": gaussian(arg_keys[10], (CA, CA), CA ** -0.5, 0.5),
        "atom_pool": gaussian(arg_keys[11], (CA, CS), CA ** -0.5, 0.5),
        "token_gain": jnp.clip(1.0 + 0.18 * jax.random.normal(arg_keys[12], (CS,), jnp.float32), 0.1, 1.9),
        "token_proj": gaussian(arg_keys[13], (CS, 4 * CS), CS ** -0.5, 0.21875),
        "token_exit": gaussian(arg_keys[14], (CS, CS), CS ** -0.5, 0.21875),
        "chain_bias": draw_chain_bias(jax.random.fold_in(arg_keys[17], 71), 0),
        "token_back": gaussian(arg_keys[16], (CS, CA), CS ** -0.5, 0.21875),
    }


EPS = 1e-05

def standardize(features):
    features = features.astype(jnp.float32)
    center = features - lax.optimization_barrier(jnp.mean(features, axis=-1, keepdims=True))
    spread = lax.optimization_barrier(jnp.mean(center * center, axis=-1, keepdims=True))
    return center * lax.rsqrt(spread + EPS)

def normalize(features, gain_vec):
    return standardize(features) * gain_vec.astype(jnp.float32)

def rounded(features):
    return lax.optimization_barrier(features.astype(jnp.bfloat16)).astype(jnp.float32)

def pair_part(pair_rows_in, pair_up, pair_down, bias_heads):
    normed = rounded(standardize(pair_rows_in))
    mixed_up = jnp.einsum('ijc,cf->ijf', normed, pair_up.astype(jnp.float32))
    hidden = rounded(jax.nn.silu(mixed_up[..., :PH]) * mixed_up[..., PH:])
    updated = pair_rows_in.astype(jnp.float32) + jnp.einsum('ijf,fc->ijc', hidden, pair_down.astype(jnp.float32))
    normed_two = rounded(standardize(updated))
    return jnp.einsum('ijc,ch->hij', normed_two, bias_heads.astype(jnp.float32)).astype(jnp.bfloat16)

def reference(pair_tensor, token_single, atom_single, atom_token, chain_index, pair_up, pair_down, bias_heads, atom_gain, atom_proj, atom_exit, atom_pool, token_gain, token_proj, token_exit, chain_bias, token_back):
    row_block = TOK_R // 4
    stacked = pair_tensor.reshape(TOKENS // row_block, row_block, TOKENS, CZ)
    mapped = lax.map(lambda part_rows: pair_part(part_rows, pair_up, pair_down, bias_heads), stacked)
    pair_bias = jnp.transpose(mapped, (1, 0, 2, 3)).reshape(HB, TOKENS, TOKENS)
    atom_normed = normalize(atom_single, atom_gain).astype(jnp.bfloat16)
    atom_projected = jnp.dot(atom_normed, atom_proj, preferred_element_type=jnp.float32)
    atom_qkv = atom_projected[:, :3 * CA].astype(jnp.bfloat16)
    atom_gate = atom_projected[:, 3 * CA:]
    blocks = ATOMS // QB
    starts = QB * jnp.arange(blocks, dtype=jnp.int32)
    positions = starts[:, None] - EDGE + jnp.arange(KW, dtype=jnp.int32)[None, :]
    in_range = (positions >= 0) & (positions < ATOMS)
    clipped = jnp.clip(positions, 0, ATOMS - 1).astype(jnp.int32)
    query_heads = atom_qkv[:, :CA].reshape(blocks, QB, HA, HDA).astype(jnp.float32)
    keys_win = atom_qkv[clipped, CA:2 * CA].reshape(blocks, KW, HA, HDA).astype(jnp.float32)
    vals_win = atom_qkv[clipped, 2 * CA:].reshape(blocks, KW, HA, HDA).astype(jnp.float32)
    query_tok = atom_token.reshape(blocks, QB)
    key_tok = atom_token[clipped]
    bias_tile = pair_bias[:HA][:, query_tok[:, :, None], key_tok[:, None, :]]
    bias_tile = jnp.transpose(bias_tile, (1, 0, 2, 3)).astype(jnp.float32)
    scores = jnp.einsum('bihd,bjhd->bhij', query_heads, keys_win) * HDA ** (-0.5) + bias_tile
    scores = jnp.where(in_range[:, None, None, :], scores, -1e+30)
    row_top = lax.optimization_barrier(jnp.max(scores, axis=-1, keepdims=True))
    weights_full = jnp.exp(scores - row_top)
    denominator = lax.optimization_barrier(jnp.sum(weights_full, axis=-1))
    attended = jnp.einsum('bhij,bjhd->bihd', rounded(weights_full), vals_win)
    attended = attended / jnp.transpose(denominator, (0, 2, 1))[..., None]
    attended = attended.reshape(ATOMS, CA)
    atom_gated = (attended * jax.nn.sigmoid(atom_gate)).astype(jnp.bfloat16)
    atom_mid = (atom_single.astype(jnp.float32) + jnp.dot(atom_gated, atom_exit, preferred_element_type=jnp.float32)).astype(jnp.bfloat16)
    atom_pooled = jax.nn.relu(jnp.dot(atom_mid, atom_pool, preferred_element_type=jnp.float32)).astype(jnp.bfloat16)
    sums = jax.ops.segment_sum(atom_pooled.astype(jnp.float32), atom_token, num_segments=TOKENS)
    counts = jax.ops.segment_sum(jnp.ones((ATOMS,), jnp.float32), atom_token, num_segments=TOKENS)
    token_mid = (token_single.astype(jnp.float32) + sums / counts[:, None]).astype(jnp.bfloat16)
    token_normed = normalize(token_mid, token_gain).astype(jnp.bfloat16)
    token_projected = jnp.dot(token_normed, token_proj, preferred_element_type=jnp.float32)
    queries = token_projected[:, :CS].astype(jnp.bfloat16)
    token_gate = token_projected[:, CS:2 * CS]
    keys_all = token_projected[:, 2 * CS:3 * CS].astype(jnp.bfloat16)
    values_all = token_projected[:, 3 * CS:].astype(jnp.bfloat16)
    same_chain = (chain_index[:, None] == chain_index[None, :]).astype(jnp.float32)

    def one_head(head_items):
        query_h, key_h, value_h, bias_h, chain_h = head_items
        head_scores = jnp.dot(query_h, key_h.T, preferred_element_type=jnp.float32) * HDT ** (-0.5) + bias_h.astype(jnp.float32) + chain_h * same_chain
        head_top = lax.optimization_barrier(jnp.max(head_scores, axis=-1, keepdims=True))
        head_exp = jnp.exp(head_scores - head_top)
        head_den = lax.optimization_barrier(jnp.sum(head_exp, axis=-1))
        return jnp.dot(head_exp.astype(jnp.bfloat16), value_h, preferred_element_type=jnp.float32) / head_den[:, None]
    heads_out = lax.map(one_head, (jnp.transpose(queries.reshape(TOKENS, HT, HDT), (1, 0, 2)), jnp.transpose(keys_all.reshape(TOKENS, HT, HDT), (1, 0, 2)), jnp.transpose(values_all.reshape(TOKENS, HT, HDT), (1, 0, 2)), pair_bias[HA:], chain_bias.astype(jnp.float32)))
    token_attended = jnp.transpose(heads_out, (1, 0, 2)).reshape(TOKENS, CS)
    token_gated = (token_attended * jax.nn.sigmoid(token_gate)).astype(jnp.bfloat16)
    token_update = (token_mid.astype(jnp.float32) + jnp.dot(token_gated, token_exit, preferred_element_type=jnp.float32)).astype(jnp.bfloat16)
    token_sent = jnp.dot(token_update, token_back, preferred_element_type=jnp.float32).astype(jnp.bfloat16)
    atom_update = (atom_mid.astype(jnp.float32) + token_sent[atom_token].astype(jnp.float32)).astype(jnp.bfloat16)
    return (token_update, atom_update)
```

```python
import functools

import jax
import jax.numpy as jnp
from jax import lax
from jax.experimental import pallas as pl
from jax.experimental.pallas import tpu as pltpu
from jax.sharding import PartitionSpec as P

CZ = 128
CS = 768
CA = 128
HT = 16
HA = 4
PH = 256
QB = 32
KW = 128
EDGE = 48
HDA = 32
HDT = 48
HB = 20

EPS = 1e-05
F32 = jnp.float32
BF16 = jnp.bfloat16


def standardize(features):
    features = features.astype(F32)
    center = features - jnp.mean(features, axis=-1, keepdims=True)
    spread = jnp.mean(center * center, axis=-1, keepdims=True)
    return center * lax.rsqrt(spread + EPS)


def dot(a, b):
    return jnp.dot(a, b, preferred_element_type=F32)


def dot_nt(a, b):
    return lax.dot_general(a, b, (((1,), (1,)), ((), ())), preferred_element_type=F32)


def pair_rows(x, up, down, heads):
    normed = standardize(x).astype(BF16)
    mixed = dot(normed, up)
    half = mixed[:, :PH]
    hidden = ((half + half * jnp.tanh(half)) * mixed[:, PH:]).astype(BF16)
    updated = x.astype(F32) + dot(hidden, down)
    return dot_nt(heads, standardize(updated).astype(BF16))


def pair_kernel(sub, x_ref, up_ref, down_ref, heads_ref, atom_ref, token_ref, stage):
    rows, cols, _ = x_ref.shape
    for at in range(0, rows, sub):
        x = x_ref[at : at + sub].reshape(sub * cols, CZ)
        found = pair_rows(x, up_ref[...], down_ref[...], heads_ref[...])
        for i in range(sub):
            stage[:, at + i, :] = found[:, i * cols : (i + 1) * cols]
    token_ref[...] = stage[:HT].astype(BF16)
    atom_ref[...] = stage[HT : HT + HA].astype(BF16)


def pair_bias(pair_tensor, pair_up, pair_down, bias_heads):
    tok_rows, tok_cols, _ = pair_tensor.shape
    tile = 16
    up = jnp.concatenate([pair_up[:, :PH] * 0.5, pair_up[:, PH:]], axis=1).astype(BF16)
    heads = jnp.zeros((32, CZ), BF16)
    heads = heads.at[:HT].set(bias_heads[:, HA:].T).at[HT : HT + HA].set(bias_heads[:, :HA].T)
    pairs = tok_rows * tok_cols
    return pl.pallas_call(
        functools.partial(pair_kernel, 4),
        grid=(tok_rows // tile,),
        in_specs=[
            pl.BlockSpec((tile, tok_cols, CZ), lambda i: (i, 0, 0)),
            pl.BlockSpec((CZ, 2 * PH), lambda i: (0, 0)),
            pl.BlockSpec((PH, CZ), lambda i: (0, 0)),
            pl.BlockSpec((32, CZ), lambda i: (0, 0)),
        ],
        out_specs=[
            pl.BlockSpec((HA, tile, tok_cols), lambda i: (0, i, 0)),
            pl.BlockSpec((HT, tile, tok_cols), lambda i: (0, i, 0)),
        ],
        out_shape=[
            jax.ShapeDtypeStruct((HA, tok_rows, tok_cols), BF16),
            jax.ShapeDtypeStruct((HT, tok_rows, tok_cols), BF16),
        ],
        scratch_shapes=[pltpu.VMEM((32, tile, tok_cols), F32)],
        compiler_params=pltpu.CompilerParams(vmem_limit_bytes=32 * 1024 * 1024),
        cost_estimate=pl.CostEstimate(
            flops=2 * pairs * (2 * CZ * PH + PH * CZ + CZ * HB),
            bytes_accessed=2 * pairs * (CZ + HB),
            transcendentals=pairs * PH,
        ),
    )(pair_tensor, up, pair_down, heads)


def with_halo(cells, axes, width):
    count = lax.axis_size(axes)
    ends = count - 1
    head, tail = cells[:width], cells[-width:]
    return jnp.concatenate(
        [
            lax.ppermute(tail, axes, [(i, i + 1) for i in range(ends)]),
            cells,
            lax.ppermute(head, axes, [(i + 1, i) for i in range(ends)]),
        ],
        axis=0,
    )


def local(
    pair_tensor,
    token_single,
    atom_single,
    atom_token,
    chain_index,
    pair_up,
    pair_down,
    bias_heads,
    atom_gain,
    atom_proj,
    atom_exit,
    atom_pool,
    token_gain,
    token_proj,
    token_exit,
    chain_bias,
    token_back,
):
    tok_rows = token_single.shape[0]
    tok_cols = pair_tensor.shape[1]
    tokens = chain_index.shape[0]
    atom_rows = atom_single.shape[0]
    atoms = atom_token.shape[0]
    col_count = lax.axis_size("col")
    row_index = lax.axis_index("row")
    col_index = lax.axis_index("col")
    row_start = row_index * tok_rows
    own = tok_rows // col_count
    own_start = row_start + col_index * own
    atom_base = (row_index * col_count + col_index) * atom_rows

    atom_normed = (standardize(atom_single) * atom_gain).astype(BF16)
    projected = dot(atom_normed, atom_proj)
    queries = projected[:, :CA].astype(BF16)
    keyvals = projected[:, CA : 3 * CA].astype(BF16)
    atom_gate = projected[:, 3 * CA :]
    extended = with_halo(keyvals, ("row", "col"), EDGE)

    atom_bias, token_bias = pair_bias(pair_tensor, pair_up, pair_down, bias_heads)
    own_bias = lax.all_to_all(token_bias, "col", split_axis=1, concat_axis=2, tiled=True)
    band = lax.all_gather(atom_bias, "col", axis=2, tiled=True)

    wide = tok_rows + 2 * tok_cols
    first_key = jnp.clip(row_start - tok_cols, 0, tokens - wide)
    band = lax.dynamic_slice_in_dim(band, first_key, wide, axis=2)
    reach = atom_rows + 2 * EDGE
    key_pos = jnp.arange(reach, dtype=jnp.int32) - EDGE
    key_tok = lax.dynamic_slice_in_dim(jnp.pad(atom_token, EDGE, mode="edge"), atom_base, reach)
    query_tok = lax.dynamic_slice_in_dim(atom_token, atom_base, atom_rows)
    block = QB * (jnp.arange(atom_rows, dtype=jnp.int32) // QB)
    valid = (
        (key_pos[None, :] >= block[:, None] - EDGE)
        & (key_pos[None, :] < block[:, None] - EDGE + KW)
        & (key_pos[None, :] + atom_base >= 0)
        & (key_pos[None, :] + atom_base < atoms)
    )
    q_hot = (query_tok[:, None] - row_start == jnp.arange(tok_rows)[None, :]).astype(BF16)
    k_hot = (key_tok[None, :] - first_key == jnp.arange(wide)[:, None]).astype(BF16)
    outs = []
    for h in range(HA):
        at = slice(h * HDA, (h + 1) * HDA)
        tile = dot(dot(q_hot, band[h]).astype(BF16), k_hot)
        scores = dot_nt(queries[:, at], extended[:, :CA][:, at]) * HDA ** (-0.5) + tile
        scores = jnp.where(valid, scores, -1e30)
        weights = jnp.exp(scores - jnp.max(scores, axis=-1, keepdims=True))
        total = jnp.sum(weights, axis=-1, keepdims=True)
        outs.append(dot(weights.astype(BF16), extended[:, CA:][:, at]) / total)
    attended = jnp.concatenate(outs, axis=1)
    atom_gated = (attended * jax.nn.sigmoid(atom_gate)).astype(BF16)
    atom_mid = (atom_single.astype(F32) + dot(atom_gated, atom_exit)).astype(BF16)

    row_mid = lax.all_gather(atom_mid, "col", axis=0, tiled=True)
    row_pooled = jax.nn.relu(dot(row_mid, atom_pool)).astype(BF16)
    row_tok = lax.dynamic_slice_in_dim(atom_token, row_index * atom_rows * col_count, atom_rows * col_count)
    pool_hot = row_tok[None, :] - own_start == jnp.arange(own)[:, None]
    counts = jnp.sum(pool_hot.astype(F32), axis=1, keepdims=True)
    pooled = dot(pool_hot.astype(BF16), row_pooled) / counts
    single = lax.dynamic_slice_in_dim(token_single, col_index * own, own)
    token_mid = (single.astype(F32) + pooled).astype(BF16)
    token_normed = (standardize(token_mid) * token_gain).astype(BF16)
    every = lax.all_gather(token_normed, ("row", "col"), axis=0, tiled=True)

    own_proj = dot(token_normed, token_proj[:, : 2 * CS])
    query = own_proj[:, :CS].astype(BF16)
    token_gate = own_proj[:, CS:]
    keyval = dot(every, token_proj[:, 2 * CS :]).astype(BF16)
    of_head = jnp.arange(CS)[None, :] // HDT == jnp.arange(HT)[:, None]
    spread = jnp.where(of_head[:, None, :], query[None], jnp.zeros((), BF16)).reshape(HT * own, CS)
    own_chain = lax.dynamic_slice_in_dim(chain_index, own_start, own)
    same = (own_chain[:, None] == chain_index[None, :]).astype(F32)
    scores = (
        (dot_nt(spread, keyval[:, :CS]) * HDT ** (-0.5)).reshape(HT, own, tokens)
        + own_bias.astype(F32)
        + chain_bias[:, None, None] * same[None]
    )
    weights = jnp.exp(scores - jnp.max(scores, axis=-1, keepdims=True))
    total = jnp.sum(weights, axis=-1, keepdims=True)
    mixed = dot(weights.astype(BF16).reshape(HT * own, tokens), keyval[:, CS:]).reshape(HT, own, CS)
    token_attended = jnp.sum(jnp.where(of_head[:, None, :], mixed / total, 0.0), axis=0)
    token_gated = (token_attended * jax.nn.sigmoid(token_gate)).astype(BF16)
    own_update = (token_mid.astype(F32) + dot(token_gated, token_exit)).astype(BF16)

    token_update = lax.all_gather(own_update, "col", axis=0, tiled=True)
    token_sent = dot(token_update, token_back).astype(BF16)
    atom_update = (atom_mid.astype(F32) + dot(q_hot, token_sent)).astype(BF16)
    return (token_update, atom_update)


def solution(mesh):
    placed = (
        P("row", "col", None),
        P("row", None),
        P(("row", "col"), None),
    ) + (P(),) * 14
    return jax.shard_map(
        local,
        mesh=mesh,
        in_specs=placed,
        out_specs=(P("row", None), P(("row", "col"), None)),
        check_vma=False,
    )
```

```python
import functools

import jax
import jax.numpy as jnp
from jax import lax
from jax.experimental import pallas as pl
from jax.experimental.pallas import tpu as pltpu
from jax.sharding import PartitionSpec as P

CZ = 128
CS = 768
CA = 128
HT = 16
HA = 4
PH = 256
QB = 32
KW = 128
EDGE = 48
HDA = 32
HDT = 48
HB = 20

EPS = 1e-05
F32 = jnp.float32
BF16 = jnp.bfloat16


def standardize(features):
    features = features.astype(F32)
    center = features - jnp.mean(features, axis=-1, keepdims=True)
    spread = jnp.mean(center * center, axis=-1, keepdims=True)
    return center * lax.rsqrt(spread + EPS)


def dot(a, b):
    return jnp.dot(a, b, preferred_element_type=F32)


def dot_nt(a, b):
    return lax.dot_general(a, b, (((1,), (1,)), ((), ())), preferred_element_type=F32)


def pair_up_part(x, up):
    return dot(standardize(x).astype(BF16), up)


def pair_down_part(x, mixed, down):
    half = mixed[:, :PH]
    hidden = ((half + half * jnp.tanh(half)) * mixed[:, PH:]).astype(BF16)
    return x.astype(F32) + dot(hidden, down)


def pair_kernel(sub, x_ref, up_ref, down_ref, heads_ref, atom_ref, token_ref, stage):
    rows, cols, _ = x_ref.shape
    groups = rows // sub

    def load(g):
        return x_ref[g * sub : (g + 1) * sub].reshape(sub * cols, CZ)

    mixed, updated = {}, {}
    for step in range(groups + 2):
        if step < groups:
            mixed[step] = pair_up_part(load(step), up_ref[...])
        g = step - 1
        if 0 <= g < groups:
            updated[g] = pair_down_part(load(g), mixed.pop(g), down_ref[...])
        g = step - 2
        if 0 <= g < groups:
            found = dot_nt(heads_ref[...], standardize(updated.pop(g)).astype(BF16))
            for i in range(sub):
                stage[:, g * sub + i, :] = found[:, i * cols : (i + 1) * cols]
    token_ref[...] = stage[:HT].astype(BF16)
    atom_ref[...] = stage[HT : HT + HA].astype(BF16)


def pair_bias(pair_tensor, pair_up, pair_down, bias_heads):
    tok_rows, tok_cols, _ = pair_tensor.shape
    tile = 32
    up = jnp.concatenate([pair_up[:, :PH] * 0.5, pair_up[:, PH:]], axis=1).astype(BF16)
    heads = jnp.zeros((32, CZ), BF16)
    heads = heads.at[:HT].set(bias_heads[:, HA:].T).at[HT : HT + HA].set(bias_heads[:, :HA].T)
    pairs = tok_rows * tok_cols
    return pl.pallas_call(
        functools.partial(pair_kernel, 2),
        grid=(tok_rows // tile,),
        in_specs=[
            pl.BlockSpec((tile, tok_cols, CZ), lambda i: (i, 0, 0)),
            pl.BlockSpec((CZ, 2 * PH), lambda i: (0, 0)),
            pl.BlockSpec((PH, CZ), lambda i: (0, 0)),
            pl.BlockSpec((32, CZ), lambda i: (0, 0)),
        ],
        out_specs=[
            pl.BlockSpec((HA, tile, tok_cols), lambda i: (0, i, 0)),
            pl.BlockSpec((HT, tile, tok_cols), lambda i: (0, i, 0)),
        ],
        out_shape=[
            jax.ShapeDtypeStruct((HA, tok_rows, tok_cols), BF16),
            jax.ShapeDtypeStruct((HT, tok_rows, tok_cols), BF16),
        ],
        scratch_shapes=[pltpu.VMEM((32, tile, tok_cols), F32)],
        compiler_params=pltpu.CompilerParams(vmem_limit_bytes=32 * 1024 * 1024),
        cost_estimate=pl.CostEstimate(
            flops=2 * pairs * (2 * CZ * PH + PH * CZ + CZ * HB),
            bytes_accessed=2 * pairs * (CZ + HB),
            transcendentals=pairs * PH,
        ),
    )(pair_tensor, up, pair_down, heads)


FAR = 1 << 20
MESH = pl.DeviceIdType.MESH


def after_kernel(
    nrow,
    ncol,
    atom_bias,
    token_bias,
    proj_hbm,
    exit_hbm,
    queries,
    atom_gate,
    keys,
    vals,
    atom_single,
    query_tok,
    key_tok,
    row_tok,
    own_chain,
    all_chain,
    single,
    of_head,
    atom_exit,
    atom_pool,
    token_gain,
    chain_rows,
    token_back,
    token_out,
    atom_out,
    band,
    own_bias,
    mids,
    every,
    updates,
    proj,
    exit_w,
    local_sem,
    band_send,
    band_pass,
    band_recv,
    bias_sem,
    mid_sem,
    tok_send,
    tok_recv,
    pass_send,
    pass_recv,
    upd_sem,
):
    r, c = lax.axis_index("row"), lax.axis_index("col")
    side = lax.rem(c, 2)
    partner = c + 1 - 2 * side
    half = ncol // 2
    tok_rows, tok_cols = band.shape[2:]
    slots = band.shape[0]
    ratio = tok_rows // tok_cols
    own = single.shape[0]
    atom_rows = queries.shape[0]
    tokens = all_chain.shape[1]

    def send(src, dst, send_sem, recv_sem, row, col):
        return pltpu.make_async_remote_copy(
            src_ref=src,
            dst_ref=dst,
            send_sem=send_sem,
            recv_sem=recv_sem,
            device_id=(row, col),
            device_id_type=MESH,
        )

    barrier = pltpu.get_barrier_semaphore()
    for k in range(1, ncol):
        pl.semaphore_signal(barrier, inc=1, device_id=(r, lax.rem(c + k, ncol)), device_id_type=MESH)
    for k in range(1, nrow):
        pl.semaphore_signal(barrier, inc=1, device_id=(lax.rem(r + k, nrow), c), device_id_type=MESH)

    loads = [
        pltpu.make_async_copy(proj_hbm, proj, local_sem.at[0]),
        pltpu.make_async_copy(exit_hbm, exit_w, local_sem.at[1]),
        pltpu.make_async_copy(
            token_bias.at[:, pl.ds(pl.multiple_of(c * own, own), own), :], own_bias.at[c], local_sem.at[2]
        ),
    ]
    for load in loads:
        load.start()

    def span(s):
        at = (s - 1) * tok_cols
        reach = QB + EDGE - 1
        low = max(0, at - reach) // 16 * 16
        high = min(tok_rows, -(-(at + tok_cols + reach) // 16) * 16)
        return low, high

    def source(s):
        col = r * ratio + s - 1
        return col, (col >= 0) & (col < ncol)

    for s in range(slots):
        low, high = span(s)
        if low > 0:
            band[s, :, 0:low, :] = jnp.zeros((HA, low, tok_cols), BF16)
        if high < tok_rows:
            band[s, :, high:tok_rows, :] = jnp.zeros((HA, tok_rows - high, tok_cols), BF16)

    pl.semaphore_wait(barrier, ncol - 1 + nrow - 1)

    def block(s):
        low, high = span(s)
        return band.at[s, :, pl.ds(low, high - low), :]

    def from_source(s, k):
        low, high = span(s)
        col = partner if k == 0 else lax.rem(c + 2 * k, ncol)
        return send(
            atom_bias.at[:, pl.ds(low, high - low), :], block(s), band_send.at[k], band_recv.at[s], r, col
        )

    def passed(s):
        return send(block(s), block(s), band_pass.at[s], band_recv.at[s], r, partner)

    def kept(s):
        low, high = span(s)
        return pltpu.make_async_copy(atom_bias.at[:, pl.ds(low, high - low), :], block(s), local_sem.at[3])

    for s in range(slots):
        col, there = source(s)

        @pl.when(c == col)
        def _():
            for k in list(range(1, half)) + [0]:
                from_source(s, k).start()
            kept(s).start()

        @pl.when(jnp.logical_not(there))
        def _():
            low, high = span(s)
            band[s, :, low:high, :] = jnp.zeros((HA, high - low, tok_cols), BF16)

    for s in range(slots):
        col, there = source(s)

        @pl.when(there & (c != col) & (lax.rem(col + 2, 2) == side))
        def _():
            passed(s).wait_recv()
            passed(s).start()

    for s in range(slots):
        col, there = source(s)

        @pl.when(there & (lax.rem(col + 2, 2) != side))
        def _():
            passed(s).wait_recv()

        @pl.when(c == col)
        def _():
            kept(s).wait()

    biases = []
    for k in range(1, ncol):
        col = lax.rem(c + k, ncol)
        biases.append(
            send(
                token_bias.at[:, pl.ds(pl.multiple_of(col * own, own), own), :],
                own_bias.at[c],
                bias_sem.at[0, k],
                bias_sem.at[1, k],
                r,
                col,
            )
        )
        biases[-1].start()

    padded = keys.shape[0]
    q_iota = lax.broadcasted_iota(jnp.int32, (atom_rows, padded), 0)
    k_iota = lax.broadcasted_iota(jnp.int32, (atom_rows, padded), 1) - EDGE
    first = jnp.bitwise_and(q_iota, -QB) - EDGE
    valid = (k_iota >= first) & (k_iota < first + KW) & (key_tok[...] > -FAR // 2)
    q_hot = (query_tok[...] == lax.broadcasted_iota(jnp.int32, (atom_rows, tok_rows), 1)).astype(F32).astype(BF16)
    k_hot = (key_tok[...] == lax.broadcasted_iota(jnp.int32, (slots * tok_cols, padded), 0)).astype(F32).astype(BF16)
    lane = lax.broadcasted_iota(jnp.int32, (1, CA), 1)
    attended = jnp.zeros((atom_rows, CA), F32)
    for h in range(HA):
        mine = ((lane >= h * HDA) & (lane < (h + 1) * HDA)).astype(F32)
        wide = jnp.concatenate([band[s, h] for s in range(slots)], axis=1)
        tile = dot(dot(q_hot, wide).astype(BF16), k_hot)
        query = (queries[...].astype(F32) * mine).astype(BF16)
        scores = dot_nt(query, keys[...]) * HDA ** (-0.5) + tile
        scores = jnp.where(valid, scores, -1e30)
        weights = jnp.exp(scores - jnp.max(scores, axis=-1, keepdims=True))
        total = jnp.sum(weights, axis=-1, keepdims=True)
        attended += dot(weights.astype(BF16), vals[...]) / total * mine
    atom_gated = (attended * jax.nn.sigmoid(atom_gate[...])).astype(BF16)
    atom_mid = (atom_single[...].astype(F32) + dot(atom_gated, atom_exit[...])).astype(BF16)
    mids[c] = atom_mid

    def gather_start(buf, sems):
        out = [send(buf.at[c], buf.at[c], sems.at[0, k], sems.at[1, k], r, lax.rem(c + 2 * k, ncol)) for k in range(1, half)]
        over = [send(buf.at[c], buf.at[c], sems.at[2, 0], sems.at[3, 0], r, partner)]
        for copy in out + over:
            copy.start()
        return out, over

    def gather_end(buf, sems, out, over):
        for k in range(1, half):
            out[k - 1].wait_recv()
            col = lax.rem(c + ncol - 2 * k, ncol)
            over.append(send(buf.at[col], buf.at[col], sems.at[2, k], sems.at[3, k], r, partner))
            over[-1].start()
        for copy in over:
            copy.wait_recv()

    out, over = gather_start(mids, mid_sem)
    sent = out + over
    gather_end(mids, mid_sem, out, over)
    sent = out + over

    row_pooled = jax.nn.relu(dot(mids[...].reshape(ncol * atom_rows, CA), atom_pool[...])).astype(BF16)
    pool_hot = (row_tok[...] == lax.broadcasted_iota(jnp.int32, (own, ncol * atom_rows), 0)).astype(F32)
    counts = jnp.sum(pool_hot, axis=1, keepdims=True)
    pooled = dot(pool_hot.astype(BF16), row_pooled) / counts
    token_mid = (single[...].astype(F32) + pooled).astype(BF16)
    token_normed = (standardize(token_mid) * token_gain[...]).astype(BF16)
    every[r, c] = token_normed

    def piece(row, col):
        return every.at[row, col]

    def along(k):
        return send(piece(r, c), piece(r, c), tok_send.at[k, 0], tok_recv.at[k, 0], r, lax.rem(c + 2 * k, ncol))

    def across(k, j):
        col = lax.rem(c + ncol - 2 * k, ncol)
        return send(piece(r, col), piece(r, col), tok_send.at[k, j], tok_recv.at[k, j], lax.rem(r + j, nrow), c)

    def over_to(k, j):
        col = lax.rem(c + ncol - 2 * k, ncol)
        row = lax.rem(r + nrow - j, nrow)
        return send(piece(row, col), piece(row, col), pass_send.at[k, j], pass_recv.at[k, j], r, partner)

    for k in range(1, half):
        along(k).start()
    for k in range(half):
        if k > 0:
            along(k).wait_recv()
        for j in range(1, nrow):
            across(k, j).start()
        over_to(k, 0).start()
    loads[0].wait()
    own_proj = dot(token_normed, proj[:, : 2 * CS])
    query = own_proj[:, :CS].astype(BF16)
    token_gate = own_proj[:, CS:]
    for k in range(half):
        for j in range(1, nrow):
            across(k, j).wait_recv()
            over_to(k, j).start()
    for k in range(half):
        for j in range(nrow):
            over_to(k, j).wait_recv()

    keyval = dot(every[...].reshape(tokens, CS), proj[:, 2 * CS :]).astype(BF16)
    spread = jnp.concatenate([query] * HT, axis=0) * of_head[...]
    same = (own_chain[...] == all_chain[...]).astype(F32)
    same = jnp.concatenate([same] * HT, axis=0) * chain_rows[...]
    loads[2].wait()
    for copy in biases:
        copy.wait_recv()
    bias = jnp.concatenate([own_bias[k].reshape(HT * own, tok_cols) for k in range(ncol)], axis=1)
    scores = dot_nt(spread, keyval[:, :CS]) * HDT ** (-0.5) + bias.astype(F32) + same
    weights = jnp.exp(scores - jnp.max(scores, axis=-1, keepdims=True))
    total = jnp.sum(weights, axis=-1, keepdims=True)
    mixed = dot(weights.astype(BF16), keyval[:, CS:]) / total * of_head[...].astype(F32)
    token_attended = jnp.sum(mixed.reshape(HT, own, CS), axis=0)
    token_gated = (token_attended * jax.nn.sigmoid(token_gate)).astype(BF16)
    loads[1].wait()
    updates[c] = (token_mid.astype(F32) + dot(token_gated, exit_w[...])).astype(BF16)

    out, over = gather_start(updates, upd_sem)
    gather_end(updates, upd_sem, out, over)
    sent = sent + out + over
    token_out[...] = updates[...]
    token_sent = dot(updates[...].reshape(tok_rows, CS), token_back[...]).astype(BF16)
    atom_out[...] = (atom_mid.astype(F32) + dot(q_hot, token_sent)).astype(BF16)

    for copy in sent + biases:
        copy.wait_send()
    for k in range(half):
        if k > 0:
            along(k).wait_send()
        for j in range(1, nrow):
            across(k, j).wait_send()
        for j in range(nrow):
            over_to(k, j).wait_send()
    for s in range(slots):
        col, there = source(s)

        @pl.when(c == col)
        def _():
            for k in range(half):
                from_source(s, k).wait_send()

        @pl.when(there & (c != col) & (lax.rem(col + 2, 2) == side))
        def _():
            passed(s).wait_send()


def with_halo(cells, axes, width):
    count = lax.axis_size(axes)
    ends = count - 1
    head, tail = cells[:width], cells[-width:]
    return jnp.concatenate(
        [
            lax.ppermute(tail, axes, [(i, i + 1) for i in range(ends)]),
            cells,
            lax.ppermute(head, axes, [(i + 1, i) for i in range(ends)]),
        ],
        axis=0,
    )


def local(
    pair_tensor,
    token_single,
    atom_single,
    atom_token,
    chain_index,
    pair_up,
    pair_down,
    bias_heads,
    atom_gain,
    atom_proj,
    atom_exit,
    atom_pool,
    token_gain,
    token_proj,
    token_exit,
    chain_bias,
    token_back,
):
    tok_rows = token_single.shape[0]
    tok_cols = pair_tensor.shape[1]
    atom_rows = atom_single.shape[0]
    col_count = lax.axis_size("col")
    row_index = lax.axis_index("row")
    col_index = lax.axis_index("col")
    row_start = row_index * tok_rows
    own = tok_rows // col_count
    own_start = row_start + col_index * own
    atom_base = (row_index * col_count + col_index) * atom_rows

    atom_normed = (standardize(atom_single) * atom_gain).astype(BF16)
    projected = dot(atom_normed, atom_proj)
    queries = projected[:, :CA].astype(BF16)
    keyvals = projected[:, CA : 3 * CA].astype(BF16)
    atom_gate = projected[:, 3 * CA :]
    extended = with_halo(keyvals, ("row", "col"), EDGE)

    atom_bias, token_bias = pair_bias(pair_tensor, pair_up, pair_down, bias_heads)

    reach = atom_rows + 2 * EDGE
    padded = -(-reach // 128) * 128
    grown = jnp.pad(extended, ((0, padded - reach), (0, 0)))
    near = jnp.pad(atom_token, (EDGE, EDGE + padded - reach), constant_values=-FAR)
    key_tok = lax.dynamic_slice_in_dim(near, atom_base, padded) - (row_start - tok_cols)
    query_tok = lax.dynamic_slice_in_dim(atom_token, atom_base, atom_rows) - row_start
    row_atoms = atom_rows * col_count
    row_tok = lax.dynamic_slice_in_dim(atom_token, row_index * row_atoms, row_atoms) - own_start
    own_chain = lax.dynamic_slice_in_dim(chain_index, own_start, own)
    single = lax.dynamic_slice_in_dim(token_single, col_index * own, own)
    of_head = jnp.arange(CS)[None, :] // HDT == jnp.arange(HT * own)[:, None] // own
    row_count = lax.axis_size("row")
    slots = tok_rows // tok_cols + 2
    half = col_count // 2
    vmem = pl.BlockSpec(memory_space=pltpu.VMEM)
    anywhere = pl.BlockSpec(memory_space=pl.ANY)
    dma = pltpu.SemaphoreType.DMA
    token_update, atom_update = pl.pallas_call(
        functools.partial(after_kernel, row_count, col_count),
        in_specs=[anywhere] * 4 + [vmem] * 17,
        out_specs=[vmem, vmem],
        out_shape=[
            jax.ShapeDtypeStruct((col_count, own, CS), BF16),
            jax.ShapeDtypeStruct((atom_rows, CA), BF16),
        ],
        scratch_shapes=[
            pltpu.VMEM((slots, HA, tok_rows, tok_cols), BF16),
            pltpu.VMEM((col_count, HT, own, tok_cols), BF16),
            pltpu.VMEM((col_count, atom_rows, CA), BF16),
            pltpu.VMEM((row_count, col_count, own, CS), BF16),
            pltpu.VMEM((col_count, own, CS), BF16),
            pltpu.VMEM(token_proj.shape, BF16),
            pltpu.VMEM(token_exit.shape, BF16),
            dma((4,)),
            dma((half,)),
            dma((slots,)),
            dma((slots,)),
            dma((2, col_count)),
            dma((4, half)),
            dma((half, row_count)),
            dma((half, row_count)),
            dma((half, row_count)),
            dma((half, row_count)),
            dma((4, half)),
        ],
        compiler_params=pltpu.CompilerParams(
            collective_id=0, has_side_effects=True, vmem_limit_bytes=52 * 1024 * 1024
        ),
    )(
        atom_bias,
        token_bias,
        token_proj,
        token_exit,
        queries,
        atom_gate,
        grown[:, :CA],
        grown[:, CA:],
        atom_single,
        query_tok[:, None],
        key_tok[None, :],
        row_tok[None, :],
        own_chain[:, None],
        chain_index[None, :],
        single,
        of_head.astype(BF16),
        atom_exit,
        atom_pool,
        token_gain[None, :],
        jnp.repeat(chain_bias, own)[:, None],
        token_back,
    )
    return (token_update.reshape(tok_rows, CS), atom_update)


def solution(mesh):
    placed = (
        P("row", "col", None),
        P("row", None),
        P(("row", "col"), None),
    ) + (P(),) * 14
    return jax.shard_map(
        local,
        mesh=mesh,
        in_specs=placed,
        out_specs=(P("row", None), P(("row", "col"), None)),
        check_vma=False,
    )
```

```python
import functools

import jax
import jax.numpy as jnp
from jax import lax
from jax.experimental import pallas as pl
from jax.experimental.pallas import tpu as pltpu
from jax.sharding import PartitionSpec as P

CZ = 128
CS = 768
CA = 128
HT = 16
HA = 4
PH = 256
QB = 32
KW = 128
EDGE = 48
HDA = 32
HDT = 48
HB = 20

EPS = 1e-05
F32 = jnp.float32
BF16 = jnp.bfloat16


def standardize(features):
    features = features.astype(F32)
    center = features - jnp.mean(features, axis=-1, keepdims=True)
    spread = jnp.mean(center * center, axis=-1, keepdims=True)
    return center * lax.rsqrt(spread + EPS)


def dot(a, b):
    return jnp.dot(a, b, preferred_element_type=F32)


def dot_nt(a, b):
    return lax.dot_general(a, b, (((1,), (1,)), ((), ())), preferred_element_type=F32)


def pair_up_part(x, up):
    return dot(standardize(x).astype(BF16), up)


def pair_down_part(x, mixed, down):
    half = mixed[:, :PH]
    hidden = ((half + half * jnp.tanh(half)) * mixed[:, PH:]).astype(BF16)
    return x.astype(F32) + dot(hidden, down)


FAR = 1 << 20
MESH = pl.DeviceIdType.MESH
VMEM_LIMIT = 58 * 1024 * 1024


def send(src, dst, send_sem, recv_sem, row, col):
    return pltpu.make_async_remote_copy(
        src_ref=src,
        dst_ref=dst,
        send_sem=send_sem,
        recv_sem=recv_sem,
        device_id=(row, col),
        device_id_type=MESH,
    )


def band_span(s, tok_rows, tok_cols, unit):
    at = (s - 1) * tok_cols
    reach = QB + EDGE - 1
    low = max(0, at - reach) // unit * unit
    high = min(tok_rows, -(-(at + tok_cols + reach) // unit) * unit)
    return low, high


def pair_kernel(
    ncol,
    sub,
    pair,
    up_ref,
    down_ref,
    heads_ref,
    own_bias,
    band,
    cells,
    up,
    stage,
    token_buf,
    atom_buf,
    cell_sem,
    bias_send,
    bias_recv,
    band_send,
    band_pass,
    band_recv,
    keep_sem,
):
    r, c = lax.axis_index("row"), lax.axis_index("col")
    side = lax.rem(c, 2)
    partner = c + 1 - 2 * side
    half = ncol // 2
    slots, _, tok_rows, tok_cols = band.shape
    ratio = tok_rows // tok_cols
    own = tok_rows // ncol
    groups = own // sub

    barrier = pltpu.get_barrier_semaphore()
    for k in range(1, ncol):
        pl.semaphore_signal(barrier, inc=1, device_id=(r, lax.rem(c + k, ncol)), device_id_type=MESH)

    def fetch(i):
        at = pl.multiple_of(lax.rem(c + 1 + i, ncol) * own, own)
        slot = lax.rem(i, 2)
        return pltpu.make_async_copy(pair.at[pl.ds(at, own)], cells.at[slot], cell_sem.at[slot])

    fetch(0).start()
    up[:, :PH] = (up_ref[:, :PH].astype(F32) * 0.5).astype(BF16)
    up[:, PH:] = up_ref[:, PH:]
    pl.semaphore_wait(barrier, ncol - 1)

    def source(s):
        col = r * ratio + s - 1
        return col, (col >= 0) & (col < ncol)

    def chunk(i):
        peer = lax.rem(c + 1 + i, ncol)
        return peer, pl.multiple_of(peer * own, own)

    def own_copy(i):
        return pltpu.make_async_copy(token_buf.at[i], own_bias.at[c], keep_sem.at[0])

    def peer_copy(i):
        peer, _ = chunk(i)
        return send(token_buf.at[i], own_bias.at[c], bias_send.at[i], bias_recv.at[i], r, peer)

    def one(i, _):
        fetch(i).wait()

        @pl.when(i + 1 < ncol)
        def _():
            fetch(i + 1).start()

        slot = lax.rem(i, 2)
        peer, at = chunk(i)

        def load(g):
            return cells[slot, g * sub : (g + 1) * sub].reshape(sub * tok_cols, CZ)

        mixed, updated = {}, {}
        for step in range(groups + 2):
            if step < groups:
                mixed[step] = pair_up_part(load(step), up[...])
            g = step - 1
            if 0 <= g < groups:
                updated[g] = pair_down_part(load(g), mixed.pop(g), down_ref[...])
            g = step - 2
            if 0 <= g < groups:
                found = dot_nt(heads_ref[...], standardize(updated.pop(g)).astype(BF16))
                for n in range(sub):
                    stage[:, g * sub + n, :] = found[:, n * tok_cols : (n + 1) * tok_cols]
        token_buf[i] = stage[HA:HB].astype(BF16)
        atom_buf[i] = stage[:HA].astype(BF16)

        for s in range(slots):
            low, high = band_span(s, tok_rows, tok_cols, own)
            col, _ = source(s)

            @pl.when((c == col) & (at >= low) & (at < high))
            def _():
                dst = band.at[s, :, pl.ds(at, own), :]
                for k in range(half):
                    to = partner if k == 0 else lax.rem(c + 2 * k, ncol)
                    send(atom_buf.at[i], dst, band_send.at[k], band_recv.at[s], r, to).start()
                pltpu.make_async_copy(atom_buf.at[i], dst, keep_sem.at[1]).start()

        @pl.when(i + 1 < ncol)
        def _():
            peer_copy(i).start()

        return 0

    lax.fori_loop(0, ncol, one, 0)
    own_copy(ncol - 1).start()

    def block(s):
        low, high = band_span(s, tok_rows, tok_cols, own)
        return band.at[s, :, pl.ds(low, high - low), :]

    def passed(s):
        return send(block(s), block(s), band_pass.at[s], band_recv.at[s], r, partner)

    for s in range(slots):
        col, there = source(s)

        @pl.when(there & (c != col) & (lax.rem(col + 2, 2) == side))
        def _():
            passed(s).wait_recv()
            passed(s).start()

    for s in range(slots):
        col, there = source(s)

        @pl.when(there & (lax.rem(col + 2, 2) != side))
        def _():
            passed(s).wait_recv()

        @pl.when(c == col)
        def _():
            pltpu.make_async_copy(block(s), block(s), keep_sem.at[1]).wait()
            for k in range(half):
                send(block(s), block(s), band_send.at[k], band_recv.at[s], r, partner).wait_send()

        @pl.when(there & (c != col) & (lax.rem(col + 2, 2) == side))
        def _():
            passed(s).wait_send()

    own_copy(ncol - 1).wait()
    for i in range(ncol - 1):
        peer_copy(i).wait()


def pair_bias(pair_tensor, pair_up, pair_down, bias_heads):
    tok_rows, tok_cols, _ = pair_tensor.shape
    ncol = lax.axis_size("col")
    own = tok_rows // ncol
    slots = tok_rows // tok_cols + 2
    pairs = tok_rows * tok_cols
    dma = pltpu.SemaphoreType.DMA
    vmem = pl.BlockSpec(memory_space=pltpu.VMEM)
    anywhere = pl.BlockSpec(memory_space=pl.ANY)
    return pl.pallas_call(
        functools.partial(pair_kernel, ncol, 2),
        in_specs=[anywhere, vmem, vmem, vmem],
        out_specs=[anywhere, anywhere],
        out_shape=[
            jax.ShapeDtypeStruct((ncol, HT, own, tok_cols), BF16),
            jax.ShapeDtypeStruct((slots, HA, tok_rows, tok_cols), BF16),
        ],
        scratch_shapes=[
            pltpu.VMEM((2, own, tok_cols, CZ), BF16),
            pltpu.VMEM((CZ, 2 * PH), BF16),
            pltpu.VMEM((HB, own, tok_cols), F32),
            pltpu.VMEM((ncol, HT, own, tok_cols), BF16),
            pltpu.VMEM((ncol, HA, own, tok_cols), BF16),
            dma((2,)),
            dma((ncol,)),
            dma((ncol,)),
            dma((ncol // 2,)),
            dma((slots,)),
            dma((slots,)),
            dma((2,)),
        ],
        compiler_params=pltpu.CompilerParams(
            collective_id=0, has_side_effects=True, vmem_limit_bytes=VMEM_LIMIT
        ),
        cost_estimate=pl.CostEstimate(
            flops=2 * pairs * (2 * CZ * PH + PH * CZ + CZ * HB),
            bytes_accessed=2 * pairs * (CZ + HB),
            transcendentals=pairs * PH,
        ),
    )(pair_tensor, pair_up, pair_down, bias_heads.T)


def after_kernel(
    nrow,
    ncol,
    bias_hbm,
    band_hbm,
    proj_hbm,
    exit_hbm,
    queries,
    atom_gate,
    keys,
    vals,
    atom_single,
    query_tok,
    key_tok,
    row_tok,
    own_chain,
    all_chain,
    single,
    atom_exit,
    atom_pool,
    token_gain,
    chain_rows,
    token_back,
    token_out,
    atom_out,
    band,
    own_bias,
    mids,
    every,
    updates,
    proj,
    exit_w,
    local_sem,
    band_sem,
    mid_sem,
    tok_send,
    tok_recv,
    pass_send,
    pass_recv,
    upd_sem,
):
    r, c = lax.axis_index("row"), lax.axis_index("col")
    side = lax.rem(c, 2)
    partner = c + 1 - 2 * side
    half = ncol // 2
    tok_rows, tok_cols = band.shape[2:]
    slots = band.shape[0]
    ratio = tok_rows // tok_cols
    own = single.shape[0]
    atom_rows = queries.shape[0]
    tokens = all_chain.shape[1]

    barrier = pltpu.get_barrier_semaphore()
    for k in range(1, half):
        pl.semaphore_signal(barrier, inc=1, device_id=(r, lax.rem(c + 2 * k, ncol)), device_id_type=MESH)
    pl.semaphore_signal(barrier, inc=1, device_id=(r, partner), device_id_type=MESH)
    for k in range(1, nrow):
        pl.semaphore_signal(barrier, inc=1, device_id=(lax.rem(r + k, nrow), c), device_id_type=MESH)

    loads = [
        pltpu.make_async_copy(proj_hbm, proj, local_sem.at[0]),
        pltpu.make_async_copy(exit_hbm, exit_w, local_sem.at[1]),
        pltpu.make_async_copy(bias_hbm, own_bias, local_sem.at[2]),
    ]
    spans = [band_span(s, tok_rows, tok_cols, own) for s in range(slots)]

    def fetched(s):
        low, high = spans[s]
        return pltpu.make_async_copy(
            band_hbm.at[s, :, pl.ds(low, high - low), :], band.at[s, :, pl.ds(low, high - low), :], band_sem.at[s]
        )

    def there(s):
        col = r * ratio + s - 1
        return (col >= 0) & (col < ncol)

    for s in range(slots):
        pl.when(there(s))(fetched(s).start)
    for load in loads:
        load.start()
    for s in range(slots):
        low, high = spans[s]
        if low > 0:
            band[s, :, 0:low, :] = jnp.zeros((HA, low, tok_cols), BF16)
        if high < tok_rows:
            band[s, :, high:tok_rows, :] = jnp.zeros((HA, tok_rows - high, tok_cols), BF16)

        @pl.when(jnp.logical_not(there(s)))
        def _():
            band[s, :, low:high, :] = jnp.zeros((HA, high - low, tok_cols), BF16)

    for s in range(slots):
        pl.when(there(s))(fetched(s).wait)

    padded = keys.shape[0]
    q_iota = lax.broadcasted_iota(jnp.int32, (atom_rows, padded), 0)
    k_iota = lax.broadcasted_iota(jnp.int32, (atom_rows, padded), 1) - EDGE
    first = jnp.bitwise_and(q_iota, -QB) - EDGE
    valid = (k_iota >= first) & (k_iota < first + KW) & (key_tok[...] > -FAR // 2)
    q_hot = (query_tok[...] == lax.broadcasted_iota(jnp.int32, (atom_rows, tok_rows), 1)).astype(F32).astype(BF16)
    k_hot = (key_tok[...] == lax.broadcasted_iota(jnp.int32, (slots * tok_cols, padded), 0)).astype(F32).astype(BF16)
    lane = lax.broadcasted_iota(jnp.int32, (1, CA), 1)
    attended = jnp.zeros((atom_rows, CA), F32)
    for h in range(HA):
        mine = ((lane >= h * HDA) & (lane < (h + 1) * HDA)).astype(F32)
        wide = jnp.concatenate([band[s, h] for s in range(slots)], axis=1)
        tile = dot(dot(q_hot, wide).astype(BF16), k_hot)
        query = (queries[...].astype(F32) * mine).astype(BF16)
        scores = dot_nt(query, keys[...]) * HDA ** (-0.5) + tile
        scores = jnp.where(valid, scores, -1e30)
        weights = jnp.exp(scores - jnp.max(scores, axis=-1, keepdims=True))
        total = jnp.sum(weights, axis=-1, keepdims=True)
        attended += dot(weights.astype(BF16), vals[...]) / total * mine
    atom_gated = (attended * jax.nn.sigmoid(atom_gate[...])).astype(BF16)
    atom_mid = (atom_single[...].astype(F32) + dot(atom_gated, atom_exit[...])).astype(BF16)
    mids[c] = atom_mid

    def gather_start(buf, sems):
        out = [send(buf.at[c], buf.at[c], sems.at[0, k], sems.at[1, k], r, lax.rem(c + 2 * k, ncol)) for k in range(1, half)]
        over = [send(buf.at[c], buf.at[c], sems.at[2, 0], sems.at[3, 0], r, partner)]
        for copy in out + over:
            copy.start()
        return out, over

    def gather_end(buf, sems, out, over):
        for k in range(1, half):
            out[k - 1].wait_recv()
            col = lax.rem(c + ncol - 2 * k, ncol)
            over.append(send(buf.at[col], buf.at[col], sems.at[2, k], sems.at[3, k], r, partner))
            over[-1].start()
        for copy in over:
            copy.wait_recv()

    pl.semaphore_wait(barrier, half + nrow - 1)
    out, over = gather_start(mids, mid_sem)
    sent = out + over
    gather_end(mids, mid_sem, out, over)
    sent = out + over

    row_pooled = jax.nn.relu(dot(mids[...].reshape(ncol * atom_rows, CA), atom_pool[...])).astype(BF16)
    pool_hot = (row_tok[...] == lax.broadcasted_iota(jnp.int32, (own, ncol * atom_rows), 0)).astype(F32)
    counts = jnp.sum(pool_hot, axis=1, keepdims=True)
    pooled = dot(pool_hot.astype(BF16), row_pooled) / counts
    token_mid = (single[...].astype(F32) + pooled).astype(BF16)
    token_normed = (standardize(token_mid) * token_gain[...]).astype(BF16)
    every[r, c] = token_normed

    def piece(row, col):
        return every.at[row, col]

    def along(k):
        return send(piece(r, c), piece(r, c), tok_send.at[k, 0], tok_recv.at[k, 0], r, lax.rem(c + 2 * k, ncol))

    def across(k, j):
        col = lax.rem(c + ncol - 2 * k, ncol)
        return send(piece(r, col), piece(r, col), tok_send.at[k, j], tok_recv.at[k, j], lax.rem(r + j, nrow), c)

    def over_to(k, j):
        col = lax.rem(c + ncol - 2 * k, ncol)
        row = lax.rem(r + nrow - j, nrow)
        return send(piece(row, col), piece(row, col), pass_send.at[k, j], pass_recv.at[k, j], r, partner)

    for k in range(1, half):
        along(k).start()
    for k in range(half):
        if k > 0:
            along(k).wait_recv()
        for j in range(1, nrow):
            across(k, j).start()
        over_to(k, 0).start()
    loads[0].wait()
    own_proj = dot(token_normed, proj[:, : 2 * CS])
    query = own_proj[:, :CS].astype(BF16)
    token_gate = own_proj[:, CS:]
    for k in range(half):
        for j in range(1, nrow):
            across(k, j).wait_recv()
            over_to(k, j).start()
    for k in range(half):
        for j in range(nrow):
            over_to(k, j).wait_recv()

    keyval = dot(every[...].reshape(tokens, CS), proj[:, 2 * CS :]).astype(BF16)
    head_at = lax.broadcasted_iota(jnp.int32, (HT, own, CS), 0) * HDT
    head_lane = lax.broadcasted_iota(jnp.int32, (HT, own, CS), 2)
    of_head = ((head_lane >= head_at) & (head_lane < head_at + HDT)).astype(F32).reshape(HT * own, CS)
    spread = jnp.concatenate([query] * HT, axis=0) * of_head.astype(BF16)
    same = (own_chain[...] == all_chain[...]).astype(F32)
    same = jnp.concatenate([same] * HT, axis=0) * chain_rows[...]
    loads[2].wait()
    bias = jnp.concatenate([own_bias[k].reshape(HT * own, tok_cols) for k in range(ncol)], axis=1)
    scores = dot_nt(spread, keyval[:, :CS]) * HDT ** (-0.5) + bias.astype(F32) + same
    weights = jnp.exp(scores - jnp.max(scores, axis=-1, keepdims=True))
    total = jnp.sum(weights, axis=-1, keepdims=True)
    mixed = dot(weights.astype(BF16), keyval[:, CS:]) / total * of_head
    token_attended = jnp.sum(mixed.reshape(HT, own, CS), axis=0)
    token_gated = (token_attended * jax.nn.sigmoid(token_gate)).astype(BF16)
    loads[1].wait()
    updates[c] = (token_mid.astype(F32) + dot(token_gated, exit_w[...])).astype(BF16)

    out, over = gather_start(updates, upd_sem)
    gather_end(updates, upd_sem, out, over)
    sent = sent + out + over
    token_out[...] = updates[...]
    token_sent = dot(updates[...].reshape(tok_rows, CS), token_back[...]).astype(BF16)
    atom_out[...] = (atom_mid.astype(F32) + dot(q_hot, token_sent)).astype(BF16)

    for copy in sent:
        copy.wait_send()
    for k in range(half):
        if k > 0:
            along(k).wait_send()
        for j in range(1, nrow):
            across(k, j).wait_send()
        for j in range(nrow):
            over_to(k, j).wait_send()


def with_halo(cells, axes, width):
    count = lax.axis_size(axes)
    ends = count - 1
    head, tail = cells[:width], cells[-width:]
    return jnp.concatenate(
        [
            lax.ppermute(tail, axes, [(i, i + 1) for i in range(ends)]),
            cells,
            lax.ppermute(head, axes, [(i + 1, i) for i in range(ends)]),
        ],
        axis=0,
    )


def local(
    pair_tensor,
    token_single,
    atom_single,
    atom_token,
    chain_index,
    pair_up,
    pair_down,
    bias_heads,
    atom_gain,
    atom_proj,
    atom_exit,
    atom_pool,
    token_gain,
    token_proj,
    token_exit,
    chain_bias,
    token_back,
):
    tok_rows = token_single.shape[0]
    tok_cols = pair_tensor.shape[1]
    atom_rows = atom_single.shape[0]
    col_count = lax.axis_size("col")
    row_index = lax.axis_index("row")
    col_index = lax.axis_index("col")
    row_start = row_index * tok_rows
    own = tok_rows // col_count
    own_start = row_start + col_index * own
    atom_base = (row_index * col_count + col_index) * atom_rows

    atom_normed = (standardize(atom_single) * atom_gain).astype(BF16)
    projected = dot(atom_normed, atom_proj)
    queries = projected[:, :CA].astype(BF16)
    keyvals = projected[:, CA : 3 * CA].astype(BF16)
    atom_gate = projected[:, 3 * CA :]
    extended = with_halo(keyvals, ("row", "col"), EDGE)

    bias, band = pair_bias(pair_tensor, pair_up, pair_down, bias_heads)

    reach = atom_rows + 2 * EDGE
    padded = -(-reach // 128) * 128
    grown = jnp.pad(extended, ((0, padded - reach), (0, 0)))
    near = jnp.pad(atom_token, (EDGE, EDGE + padded - reach), constant_values=-FAR)
    key_tok = lax.dynamic_slice_in_dim(near, atom_base, padded) - (row_start - tok_cols)
    query_tok = lax.dynamic_slice_in_dim(atom_token, atom_base, atom_rows) - row_start
    row_atoms = atom_rows * col_count
    row_tok = lax.dynamic_slice_in_dim(atom_token, row_index * row_atoms, row_atoms) - own_start
    own_chain = lax.dynamic_slice_in_dim(chain_index, own_start, own)
    single = lax.dynamic_slice_in_dim(token_single, col_index * own, own)
    row_count = lax.axis_size("row")
    slots = tok_rows // tok_cols + 2
    half = col_count // 2
    vmem = pl.BlockSpec(memory_space=pltpu.VMEM)
    anywhere = pl.BlockSpec(memory_space=pl.ANY)
    dma = pltpu.SemaphoreType.DMA
    token_update, atom_update = pl.pallas_call(
        functools.partial(after_kernel, row_count, col_count),
        in_specs=[anywhere] * 4 + [vmem] * 16,
        out_specs=[vmem, vmem],
        out_shape=[
            jax.ShapeDtypeStruct((col_count, own, CS), BF16),
            jax.ShapeDtypeStruct((atom_rows, CA), BF16),
        ],
        scratch_shapes=[
            pltpu.VMEM((slots, HA, tok_rows, tok_cols), BF16),
            pltpu.VMEM((col_count, HT, own, tok_cols), BF16),
            pltpu.VMEM((col_count, atom_rows, CA), BF16),
            pltpu.VMEM((row_count, col_count, own, CS), BF16),
            pltpu.VMEM((col_count, own, CS), BF16),
            pltpu.VMEM(token_proj.shape, BF16),
            pltpu.VMEM(token_exit.shape, BF16),
            dma((4,)),
            dma((slots,)),
            dma((4, half)),
            dma((half, row_count)),
            dma((half, row_count)),
            dma((half, row_count)),
            dma((half, row_count)),
            dma((4, half)),
        ],
        compiler_params=pltpu.CompilerParams(
            collective_id=1, has_side_effects=True, vmem_limit_bytes=VMEM_LIMIT
        ),
    )(
        bias,
        band,
        token_proj,
        token_exit,
        queries,
        atom_gate,
        grown[:, :CA],
        grown[:, CA:],
        atom_single,
        query_tok[:, None],
        key_tok[None, :],
        row_tok[None, :],
        own_chain[:, None],
        chain_index[None, :],
        single,
        atom_exit,
        atom_pool,
        token_gain[None, :],
        jnp.repeat(chain_bias, own)[:, None],
        token_back,
    )
    return (token_update.reshape(tok_rows, CS), atom_update)


def solution(mesh):
    placed = (
        P("row", "col", None),
        P("row", None),
        P(("row", "col"), None),
    ) + (P(),) * 14
    return jax.shard_map(
        local,
        mesh=mesh,
        in_specs=placed,
        out_specs=(P("row", None), P(("row", "col"), None)),
        check_vma=False,
    )
```

```python
import functools

import jax
import jax.numpy as jnp
from jax import lax
from jax.experimental import pallas as pl
from jax.experimental.pallas import tpu as pltpu
from jax.sharding import PartitionSpec as P

CZ = 128
CS = 768
CA = 128
HT = 16
HA = 4
PH = 256
QB = 32
KW = 128
EDGE = 48
HDA = 32
HDT = 48
HB = 20

EPS = 1e-05
F32 = jnp.float32
BF16 = jnp.bfloat16


def standardize(features):
    features = features.astype(F32)
    center = features - jnp.mean(features, axis=-1, keepdims=True)
    spread = jnp.mean(center * center, axis=-1, keepdims=True)
    return center * lax.rsqrt(spread + EPS)


def dot(a, b):
    return jnp.dot(a, b, preferred_element_type=F32)


def dot_nt(a, b):
    return lax.dot_general(a, b, (((1,), (1,)), ((), ())), preferred_element_type=F32)


def pair_up_part(x, up):
    return dot(standardize(x).astype(BF16), up)


def pair_down_part(x, mixed, down):
    half = mixed[:, :PH]
    hidden = ((half + half * jnp.tanh(half)) * mixed[:, PH:]).astype(BF16)
    return x.astype(F32) + dot(hidden, down)


FAR = 1 << 20
MESH = pl.DeviceIdType.MESH
VMEM_LIMIT = 58 * 1024 * 1024


def send(src, dst, send_sem, recv_sem, row, col):
    return pltpu.make_async_remote_copy(
        src_ref=src,
        dst_ref=dst,
        send_sem=send_sem,
        recv_sem=recv_sem,
        device_id=(row, col),
        device_id_type=MESH,
    )


def band_span(s, tok_rows, tok_cols, unit):
    at = (s - 1) * tok_cols
    reach = QB + EDGE - 1
    low = max(0, at - reach) // unit * unit
    high = min(tok_rows, -(-(at + tok_cols + reach) // unit) * unit)
    return low, high


def pair_kernel(
    ncol,
    sub,
    pair,
    up_ref,
    down_ref,
    heads_ref,
    own_bias,
    band,
    cells,
    up,
    stage,
    token_buf,
    atom_buf,
    cell_sem,
    bias_send,
    bias_recv,
    band_send,
    band_pass,
    band_recv,
    keep_sem,
):
    r, c = lax.axis_index("row"), lax.axis_index("col")
    side = lax.rem(c, 2)
    partner = c + 1 - 2 * side
    half = ncol // 2
    slots, _, tok_rows, tok_cols = band.shape
    ratio = tok_rows // tok_cols
    own = tok_rows // ncol
    groups = own // sub

    barrier = pltpu.get_barrier_semaphore()
    for k in range(1, ncol):
        pl.semaphore_signal(barrier, inc=1, device_id=(r, lax.rem(c + k, ncol)), device_id_type=MESH)

    def fetch(i):
        at = pl.multiple_of(lax.rem(c + 1 + i, ncol) * own, own)
        slot = lax.rem(i, 2)
        return pltpu.make_async_copy(pair.at[pl.ds(at, own)], cells.at[slot], cell_sem.at[slot])

    fetch(0).start()
    up[:, :PH] = (up_ref[:, :PH].astype(F32) * 0.5).astype(BF16)
    up[:, PH:] = up_ref[:, PH:]
    pl.semaphore_wait(barrier, ncol - 1)

    def source(s):
        col = r * ratio + s - 1
        return col, (col >= 0) & (col < ncol)

    def chunk(i):
        peer = lax.rem(c + 1 + i, ncol)
        return peer, pl.multiple_of(peer * own, own)

    def own_copy(i):
        return pltpu.make_async_copy(token_buf.at[i], own_bias.at[c], keep_sem.at[0])

    def peer_copy(i):
        peer, _ = chunk(i)
        return send(token_buf.at[i], own_bias.at[c], bias_send.at[i], bias_recv.at[i], r, peer)

    def one(i, _):
        fetch(i).wait()

        @pl.when(i + 1 < ncol)
        def _():
            fetch(i + 1).start()

        slot = lax.rem(i, 2)
        peer, at = chunk(i)

        def load(g):
            return cells[slot, g * sub : (g + 1) * sub].reshape(sub * tok_cols, CZ)

        mixed, updated = {}, {}
        for step in range(groups + 2):
            if step < groups:
                mixed[step] = pair_up_part(load(step), up[...])
            g = step - 1
            if 0 <= g < groups:
                updated[g] = pair_down_part(load(g), mixed.pop(g), down_ref[...])
            g = step - 2
            if 0 <= g < groups:
                found = dot_nt(heads_ref[...], standardize(updated.pop(g)).astype(BF16))
                for n in range(sub):
                    stage[:, g * sub + n, :] = found[:, n * tok_cols : (n + 1) * tok_cols]
        token_buf[i] = stage[HA:HB].astype(BF16)
        atom_buf[i] = stage[:HA].astype(BF16)

        for s in range(slots):
            low, high = band_span(s, tok_rows, tok_cols, own)
            col, _ = source(s)

            @pl.when((c == col) & (at >= low) & (at < high))
            def _():
                dst = band.at[s, :, pl.ds(at, own), :]
                for k in range(half):
                    to = partner if k == 0 else lax.rem(c + 2 * k, ncol)
                    send(atom_buf.at[i], dst, band_send.at[k], band_recv.at[s], r, to).start()
                pltpu.make_async_copy(atom_buf.at[i], dst, keep_sem.at[1]).start()

        @pl.when(i + 1 < ncol)
        def _():
            peer_copy(i).start()

        return 0

    lax.fori_loop(0, ncol, one, 0)
    own_copy(ncol - 1).start()

    def block(s):
        low, high = band_span(s, tok_rows, tok_cols, own)
        return band.at[s, :, pl.ds(low, high - low), :]

    def passed(s):
        return send(block(s), block(s), band_pass.at[s], band_recv.at[s], r, partner)

    for s in range(slots):
        col, there = source(s)

        @pl.when(there & (c != col) & (lax.rem(col + 2, 2) == side))
        def _():
            passed(s).wait_recv()
            passed(s).start()

    for s in range(slots):
        col, there = source(s)

        @pl.when(there & (lax.rem(col + 2, 2) != side))
        def _():
            passed(s).wait_recv()

        @pl.when(c == col)
        def _():
            pltpu.make_async_copy(block(s), block(s), keep_sem.at[1]).wait()
            for k in range(half):
                send(block(s), block(s), band_send.at[k], band_recv.at[s], r, partner).wait_send()

        @pl.when(there & (c != col) & (lax.rem(col + 2, 2) == side))
        def _():
            passed(s).wait_send()

    own_copy(ncol - 1).wait()
    for i in range(ncol - 1):
        peer_copy(i).wait()


def pair_bias(pair_tensor, pair_up, pair_down, bias_heads):
    tok_rows, tok_cols, _ = pair_tensor.shape
    ncol = lax.axis_size("col")
    own = tok_rows // ncol
    slots = tok_rows // tok_cols + 2
    pairs = tok_rows * tok_cols
    dma = pltpu.SemaphoreType.DMA
    vmem = pl.BlockSpec(memory_space=pltpu.VMEM)
    anywhere = pl.BlockSpec(memory_space=pl.ANY)
    return pl.pallas_call(
        functools.partial(pair_kernel, ncol, 2),
        in_specs=[anywhere, vmem, vmem, vmem],
        out_specs=[anywhere, anywhere],
        out_shape=[
            jax.ShapeDtypeStruct((ncol, HT, own, tok_cols), BF16),
            jax.ShapeDtypeStruct((slots, HA, tok_rows, tok_cols), BF16),
        ],
        scratch_shapes=[
            pltpu.VMEM((2, own, tok_cols, CZ), BF16),
            pltpu.VMEM((CZ, 2 * PH), BF16),
            pltpu.VMEM((HB, own, tok_cols), F32),
            pltpu.VMEM((ncol, HT, own, tok_cols), BF16),
            pltpu.VMEM((ncol, HA, own, tok_cols), BF16),
            dma((2,)),
            dma((ncol,)),
            dma((ncol,)),
            dma((ncol // 2,)),
            dma((slots,)),
            dma((slots,)),
            dma((2,)),
        ],
        compiler_params=pltpu.CompilerParams(
            collective_id=0, has_side_effects=True, vmem_limit_bytes=VMEM_LIMIT
        ),
        cost_estimate=pl.CostEstimate(
            flops=2 * pairs * (2 * CZ * PH + PH * CZ + CZ * HB),
            bytes_accessed=2 * pairs * (CZ + HB),
            transcendentals=pairs * PH,
        ),
    )(pair_tensor, pair_up, pair_down, bias_heads.T)


def after_kernel(
    nrow,
    ncol,
    bias_hbm,
    band_hbm,
    proj_hbm,
    exit_hbm,
    projected,
    grown,
    atom_single,
    query_tok,
    key_tok,
    row_tok,
    own_chain,
    all_chain,
    single,
    atom_exit,
    atom_pool,
    token_gain,
    chain_rows,
    token_back,
    token_out,
    atom_out,
    band,
    own_bias,
    mids,
    every,
    updates,
    proj,
    exit_w,
    local_sem,
    band_sem,
    mid_sem,
    tok_send,
    tok_recv,
    pass_send,
    pass_recv,
    upd_sem,
):
    r, c = lax.axis_index("row"), lax.axis_index("col")
    side = lax.rem(c, 2)
    partner = c + 1 - 2 * side
    half = ncol // 2
    tok_rows, tok_cols = band.shape[2:]
    slots = band.shape[0]
    ratio = tok_rows // tok_cols
    own = single.shape[0]
    atom_rows = atom_single.shape[0]
    tokens = all_chain.shape[1]

    barrier = pltpu.get_barrier_semaphore()
    for k in range(1, half):
        pl.semaphore_signal(barrier, inc=1, device_id=(r, lax.rem(c + 2 * k, ncol)), device_id_type=MESH)
    pl.semaphore_signal(barrier, inc=1, device_id=(r, partner), device_id_type=MESH)
    for k in range(1, nrow):
        pl.semaphore_signal(barrier, inc=1, device_id=(lax.rem(r + k, nrow), c), device_id_type=MESH)

    loads = [
        pltpu.make_async_copy(proj_hbm, proj, local_sem.at[0]),
        pltpu.make_async_copy(exit_hbm, exit_w, local_sem.at[1]),
        pltpu.make_async_copy(bias_hbm, own_bias, local_sem.at[2]),
    ]
    spans = [band_span(s, tok_rows, tok_cols, own) for s in range(slots)]

    def fetched(s):
        low, high = spans[s]
        return pltpu.make_async_copy(
            band_hbm.at[s, :, pl.ds(low, high - low), :], band.at[s, :, pl.ds(low, high - low), :], band_sem.at[s]
        )

    def there(s):
        col = r * ratio + s - 1
        return (col >= 0) & (col < ncol)

    for s in range(slots):
        pl.when(there(s))(fetched(s).start)
    for load in loads:
        load.start()
    for s in range(slots):
        low, high = spans[s]
        if low > 0:
            band[s, :, 0:low, :] = jnp.zeros((HA, low, tok_cols), BF16)
        if high < tok_rows:
            band[s, :, high:tok_rows, :] = jnp.zeros((HA, tok_rows - high, tok_cols), BF16)

        @pl.when(jnp.logical_not(there(s)))
        def _():
            band[s, :, low:high, :] = jnp.zeros((HA, high - low, tok_cols), BF16)

    for s in range(slots):
        pl.when(there(s))(fetched(s).wait)

    padded = grown.shape[0]
    q_iota = lax.broadcasted_iota(jnp.int32, (atom_rows, padded), 0)
    k_iota = lax.broadcasted_iota(jnp.int32, (atom_rows, padded), 1) - EDGE
    first = jnp.bitwise_and(q_iota, -QB) - EDGE
    valid = (k_iota >= first) & (k_iota < first + KW) & (key_tok[...] > -FAR // 2)
    q_hot = (query_tok[...] == lax.broadcasted_iota(jnp.int32, (atom_rows, tok_rows), 1)).astype(F32).astype(BF16)
    k_hot = (key_tok[...] == lax.broadcasted_iota(jnp.int32, (slots * tok_cols, padded), 0)).astype(F32).astype(BF16)
    lane = lax.broadcasted_iota(jnp.int32, (1, CA), 1)
    attended = jnp.zeros((atom_rows, CA), F32)
    for h in range(HA):
        mine = ((lane >= h * HDA) & (lane < (h + 1) * HDA)).astype(F32)
        wide = jnp.concatenate([band[s, h] for s in range(slots)], axis=1)
        tile = dot(dot(q_hot, wide).astype(BF16), k_hot)
        query = (projected[:, :CA] * mine).astype(BF16)
        scores = dot_nt(query, grown[:, :CA]) * HDA ** (-0.5) + tile
        scores = jnp.where(valid, scores, -1e30)
        weights = jnp.exp(scores - jnp.max(scores, axis=-1, keepdims=True))
        total = jnp.sum(weights, axis=-1, keepdims=True)
        attended += dot(weights.astype(BF16), grown[:, CA:]) / total * mine
    atom_gated = (attended * jax.nn.sigmoid(projected[:, 3 * CA :])).astype(BF16)
    atom_mid = (atom_single[...].astype(F32) + dot(atom_gated, atom_exit[...])).astype(BF16)
    mids[c] = atom_mid

    def gather_start(buf, sems):
        out = [send(buf.at[c], buf.at[c], sems.at[0, k], sems.at[1, k], r, lax.rem(c + 2 * k, ncol)) for k in range(1, half)]
        over = [send(buf.at[c], buf.at[c], sems.at[2, 0], sems.at[3, 0], r, partner)]
        for copy in out + over:
            copy.start()
        return out, over

    def gather_end(buf, sems, out, over):
        for k in range(1, half):
            out[k - 1].wait_recv()
            col = lax.rem(c + ncol - 2 * k, ncol)
            over.append(send(buf.at[col], buf.at[col], sems.at[2, k], sems.at[3, k], r, partner))
            over[-1].start()
        for copy in over:
            copy.wait_recv()

    pl.semaphore_wait(barrier, half + nrow - 1)
    out, over = gather_start(mids, mid_sem)
    sent = out + over
    gather_end(mids, mid_sem, out, over)
    sent = out + over

    row_pooled = jax.nn.relu(dot(mids[...].reshape(ncol * atom_rows, CA), atom_pool[...])).astype(BF16)
    pool_hot = (row_tok[...] == lax.broadcasted_iota(jnp.int32, (own, ncol * atom_rows), 0)).astype(F32)
    counts = jnp.sum(pool_hot, axis=1, keepdims=True)
    pooled = dot(pool_hot.astype(BF16), row_pooled) / counts
    token_mid = (single[...].astype(F32) + pooled).astype(BF16)
    token_normed = (standardize(token_mid) * token_gain[...]).astype(BF16)
    every[r, c] = token_normed

    def piece(row, col):
        return every.at[row, col]

    def along(k):
        return send(piece(r, c), piece(r, c), tok_send.at[k, 0], tok_recv.at[k, 0], r, lax.rem(c + 2 * k, ncol))

    def across(k, j):
        col = lax.rem(c + ncol - 2 * k, ncol)
        return send(piece(r, col), piece(r, col), tok_send.at[k, j], tok_recv.at[k, j], lax.rem(r + j, nrow), c)

    def over_to(k, j):
        col = lax.rem(c + ncol - 2 * k, ncol)
        row = lax.rem(r + nrow - j, nrow)
        return send(piece(row, col), piece(row, col), pass_send.at[k, j], pass_recv.at[k, j], r, partner)

    for k in range(1, half):
        along(k).start()
    for k in range(half):
        if k > 0:
            along(k).wait_recv()
        for j in range(1, nrow):
            across(k, j).start()
        over_to(k, 0).start()
    loads[0].wait()
    own_proj = dot(token_normed, proj[:, : 2 * CS])
    query = own_proj[:, :CS].astype(BF16)
    token_gate = own_proj[:, CS:]
    for k in range(half):
        for j in range(1, nrow):
            across(k, j).wait_recv()
            over_to(k, j).start()
    for k in range(half):
        for j in range(nrow):
            over_to(k, j).wait_recv()

    keyval = dot(every[...].reshape(tokens, CS), proj[:, 2 * CS :]).astype(BF16)
    head_at = lax.broadcasted_iota(jnp.int32, (HT, own, CS), 0) * HDT
    head_lane = lax.broadcasted_iota(jnp.int32, (HT, own, CS), 2)
    of_head = ((head_lane >= head_at) & (head_lane < head_at + HDT)).astype(F32).reshape(HT * own, CS)
    spread = jnp.concatenate([query] * HT, axis=0) * of_head.astype(BF16)
    same = (own_chain[...] == all_chain[...]).astype(F32)
    same = jnp.concatenate([same] * HT, axis=0) * chain_rows[...]
    loads[2].wait()
    bias = jnp.concatenate([own_bias[k].reshape(HT * own, tok_cols) for k in range(ncol)], axis=1)
    scores = dot_nt(spread, keyval[:, :CS]) * HDT ** (-0.5) + bias.astype(F32) + same
    weights = jnp.exp(scores - jnp.max(scores, axis=-1, keepdims=True))
    total = jnp.sum(weights, axis=-1, keepdims=True)
    mixed = dot(weights.astype(BF16), keyval[:, CS:]) / total * of_head
    token_attended = jnp.sum(mixed.reshape(HT, own, CS), axis=0)
    token_gated = (token_attended * jax.nn.sigmoid(token_gate)).astype(BF16)
    loads[1].wait()
    updates[c] = (token_mid.astype(F32) + dot(token_gated, exit_w[...])).astype(BF16)

    out, over = gather_start(updates, upd_sem)
    gather_end(updates, upd_sem, out, over)
    sent = sent + out + over
    token_out[...] = updates[...]
    token_sent = dot(updates[...].reshape(tok_rows, CS), token_back[...]).astype(BF16)
    atom_out[...] = (atom_mid.astype(F32) + dot(q_hot, token_sent)).astype(BF16)

    for copy in sent:
        copy.wait_send()
    for k in range(half):
        if k > 0:
            along(k).wait_send()
        for j in range(1, nrow):
            across(k, j).wait_send()
        for j in range(nrow):
            over_to(k, j).wait_send()


def with_halo(cells, axes, width):
    count = lax.axis_size(axes)
    ends = count - 1
    head, tail = cells[:width], cells[-width:]
    return jnp.concatenate(
        [
            lax.ppermute(tail, axes, [(i, i + 1) for i in range(ends)]),
            cells,
            lax.ppermute(head, axes, [(i + 1, i) for i in range(ends)]),
        ],
        axis=0,
    )


def local(
    pair_tensor,
    token_single,
    atom_single,
    atom_token,
    chain_index,
    pair_up,
    pair_down,
    bias_heads,
    atom_gain,
    atom_proj,
    atom_exit,
    atom_pool,
    token_gain,
    token_proj,
    token_exit,
    chain_bias,
    token_back,
):
    tok_rows = token_single.shape[0]
    tok_cols = pair_tensor.shape[1]
    atom_rows = atom_single.shape[0]
    col_count = lax.axis_size("col")
    row_index = lax.axis_index("row")
    col_index = lax.axis_index("col")
    row_start = row_index * tok_rows
    own = tok_rows // col_count
    own_start = row_start + col_index * own
    atom_base = (row_index * col_count + col_index) * atom_rows

    atom_normed = (standardize(atom_single) * atom_gain).astype(BF16)
    projected = dot(atom_normed, atom_proj)
    keyvals = projected[:, CA : 3 * CA].astype(BF16)
    extended = with_halo(keyvals, ("row", "col"), EDGE)

    bias, band = pair_bias(pair_tensor, pair_up, pair_down, bias_heads)

    reach = atom_rows + 2 * EDGE
    padded = -(-reach // 128) * 128
    grown = jnp.pad(extended, ((0, padded - reach), (0, 0)))
    near = jnp.pad(atom_token, (EDGE, EDGE + padded - reach), constant_values=-FAR)
    key_tok = lax.dynamic_slice_in_dim(near, atom_base, padded) - (row_start - tok_cols)
    query_tok = lax.dynamic_slice_in_dim(atom_token, atom_base, atom_rows) - row_start
    row_atoms = atom_rows * col_count
    row_tok = lax.dynamic_slice_in_dim(atom_token, row_index * row_atoms, row_atoms) - own_start
    own_chain = lax.dynamic_slice_in_dim(chain_index, own_start, own)
    single = lax.dynamic_slice_in_dim(token_single, col_index * own, own)
    row_count = lax.axis_size("row")
    slots = tok_rows // tok_cols + 2
    half = col_count // 2
    vmem = pl.BlockSpec(memory_space=pltpu.VMEM)
    anywhere = pl.BlockSpec(memory_space=pl.ANY)
    dma = pltpu.SemaphoreType.DMA
    token_update, atom_update = pl.pallas_call(
        functools.partial(after_kernel, row_count, col_count),
        in_specs=[anywhere] * 4 + [vmem] * 14,
        out_specs=[vmem, vmem],
        out_shape=[
            jax.ShapeDtypeStruct((col_count, own, CS), BF16),
            jax.ShapeDtypeStruct((atom_rows, CA), BF16),
        ],
        scratch_shapes=[
            pltpu.VMEM((slots, HA, tok_rows, tok_cols), BF16),
            pltpu.VMEM((col_count, HT, own, tok_cols), BF16),
            pltpu.VMEM((col_count, atom_rows, CA), BF16),
            pltpu.VMEM((row_count, col_count, own, CS), BF16),
            pltpu.VMEM((col_count, own, CS), BF16),
            pltpu.VMEM(token_proj.shape, BF16),
            pltpu.VMEM(token_exit.shape, BF16),
            dma((4,)),
            dma((slots,)),
            dma((4, half)),
            dma((half, row_count)),
            dma((half, row_count)),
            dma((half, row_count)),
            dma((half, row_count)),
            dma((4, half)),
        ],
        compiler_params=pltpu.CompilerParams(
            collective_id=1, has_side_effects=True, vmem_limit_bytes=VMEM_LIMIT
        ),
    )(
        bias,
        band,
        token_proj,
        token_exit,
        projected,
        grown,
        atom_single,
        query_tok[:, None],
        key_tok[None, :],
        row_tok[None, :],
        own_chain[:, None],
        chain_index[None, :],
        single,
        atom_exit,
        atom_pool,
        token_gain[None, :],
        jnp.repeat(chain_bias, own)[:, None],
        token_back,
    )
    return (token_update.reshape(tok_rows, CS), atom_update)


def solution(mesh):
    placed = (
        P("row", "col", None),
        P("row", None),
        P(("row", "col"), None),
    ) + (P(),) * 14
    return jax.shard_map(
        local,
        mesh=mesh,
        in_specs=placed,
        out_specs=(P("row", None), P(("row", "col"), None)),
        check_vma=False,
    )
```
